32 devices in a mesh: mol: 2 (over x), row: 16 (over z, y, core).
Axes of the slice: x: 2, y: 2, z: 4, core: 2. Of those that a mesh axis runs over, the one named last changes fastest.
Arguments:
- amplitude: float32 [32, 15, 256, 256], P(('mol', 'row')), parts along dimension 0, may hold values from -0.375 to 0.375
- integral: float32 [32, 15, 256, 256], P(('mol', 'row')), parts along dimension 0, may hold values from -6 to 6
- pair_gap: float32 [32, 256], P(('mol', 'row')), parts along dimension 0, may hold values from 0.5 to 2
- present: int32 [32, 15], P(('mol', 'row')), parts along dimension 0, may hold values from 0 to 1, as said below
Outputs:
- new_amplitude: float32 [32, 15, 256, 256], P(('mol', 'row')), parts along dimension 0
- energy: float32 [2], P('mol'), parts along dimension 0
The draws below stay inside these ranges and needn't reach their ends.
There are 2 independent parts, one for each index of `mol`. The reference program is written for one: setup_inputs(seed, part) draws one part's arguments, and reference() takes and returns one part's arrays. A program takes and returns all parts, laid end to end along the dimension named above; each array names one. Nothing has to cross between parts.
Inputs may be any that keep to these rules, and one draw needn't show every extreme that they name: Symmetric: present[I,s] equals present[I + s - 7, 14 - s]; slot 7 is always 1; slots whose column block lies outside 0 to 15 are 0; some block has every slot 1.
All inputs are finite; a program needn't handle non-finite values.
Results may differ from the reference program's by a relative error of at most 0.000053.
Values sent between devices are 32-bit elements; how exact they have to be, the bound alone decides.
No kernel may reach another device: no remote copies, remote signals or barrier semaphores. Data moves between devices by JAX's collectives and lax.ppermute only.
A program may use at most 64 MiB of HBM per device.

```python
import jax
import jax.numpy as jnp
from jax import lax

PAIRS_PER_BLOCK = 256
COUPLING_REACH = 7
SLOT_COUNT = 15
PAIR_BLOCK_COUNT = 16


def draw_present(key, part):
    key = jax.random.fold_in(key, 11)
    key_edges, key_centre = jax.random.split(key)
    edges = jax.random.randint(key_edges, (PAIR_BLOCK_COUNT, COUPLING_REACH), 0, 2)
    centre = jax.random.randint(key_centre, (), COUPLING_REACH, PAIR_BLOCK_COUNT - COUPLING_REACH)
    rows = jnp.arange(PAIR_BLOCK_COUNT)[:, None]
    offsets = jnp.arange(1, COUPLING_REACH + 1)[None, :]
    edges = jnp.where((rows == centre) | (rows + offsets == centre), 1, edges)
    edges = jnp.where(rows + offsets < PAIR_BLOCK_COUNT, edges, 0)
    source = rows - offsets
    lower = jnp.where(source >= 0, edges[jnp.clip(source, 0, PAIR_BLOCK_COUNT - 1), offsets - 1 + 0 * rows], 0)
    lower = lower[:, ::-1]
    diagonal = jnp.ones((PAIR_BLOCK_COUNT, 1), jnp.int32)
    return jnp.concatenate([lower, diagonal, edges], axis=1).astype(jnp.int32)


def level_of(own_key, dims, cuts, low, high):
    gain = 1.0
    for dim, blocks in cuts:
        steps = jax.random.uniform(jax.random.fold_in(jax.random.fold_in(own_key, 6), dim), (blocks,), jnp.float32, low / len(cuts), high / len(cuts))
        gain = gain * jnp.repeat(jnp.exp(steps), dims[dim] // blocks).reshape((-1,) + (1,) * (len(dims) - 1 - dim))
    return gain


def centred(stream_key, shape, spread, bound, pieces=(), dtype=jnp.bfloat16):
    entries = jax.random.normal(stream_key, shape, jnp.float32) * spread
    if len(pieces) > 0:
        entries = level_of(stream_key, shape, pieces, -0.22, 0.18) * entries
    return jnp.clip(entries, min=-bound, max=bound).astype(dtype)


def setup_inputs(seed: int = 0, part: int = 0) -> dict:
    seeds = jax.random.split(jax.random.key(seed), 5)
    own_keys = jax.random.split(jax.random.fold_in(seeds[4], part), 5)
    return {
        "amplitude": centred(own_keys[0], (PAIR_BLOCK_COUNT, SLOT_COUNT, PAIRS_PER_BLOCK, PAIRS_PER_BLOCK), PAIRS_PER_BLOCK ** -0.5, 0.375, ((0, 16),), jnp.float32),
        "integral": centred(own_keys[1], (PAIR_BLOCK_COUNT, SLOT_COUNT, PAIRS_PER_BLOCK, PAIRS_PER_BLOCK), 1.0, 6.0, ((0, 16),), jnp.float32),
        "pair_gap": jnp.clip(0.5 + 1.5 * jax.random.uniform(own_keys[2], (PAIR_BLOCK_COUNT, PAIRS_PER_BLOCK), jnp.float32) ** level_of(own_keys[2], (PAIR_BLOCK_COUNT, PAIRS_PER_BLOCK), ((0, 16),), -0.2, 0.2), 0.5, 2.0),
        "present": draw_present(jax.random.fold_in(jax.random.fold_in(seeds[4], part), 71), part),
    }


def cycle_terms(amp_slots, int_slots):
    hi = lax.Precision.HIGHEST
    first = jnp.einsum('sij,sjk->sik', amp_slots, int_slots, precision=hi)
    second = jnp.einsum('sij,skj->sik', amp_slots, int_slots, precision=hi)
    third = jnp.einsum('sij,skj->sik', first, amp_slots, precision=hi)
    return first + second - 0.5 * third


def reference(amplitude, integral, pair_gap, present):
    cycle = lax.map(lambda pair: cycle_terms(pair[0], pair[1]), (amplitude, integral))
    padded_cycle = jnp.pad(cycle, ((COUPLING_REACH, COUPLING_REACH), (0, 0), (0, 0), (0, 0)))
    gap_pad = jnp.pad(pair_gap, ((COUPLING_REACH, COUPLING_REACH), (0, 0)))
    mirror_list = []
    gap_list = []
    for column_slot in range(SLOT_COUNT):
        block_offset = column_slot - COUPLING_REACH
        pair_blocks = padded_cycle[COUPLING_REACH + block_offset:COUPLING_REACH + block_offset + PAIR_BLOCK_COUNT, SLOT_COUNT - 1 - column_slot]
        mirror_list.append(jnp.swapaxes(pair_blocks, 1, 2))
        gap_list.append(gap_pad[COUPLING_REACH + block_offset:COUPLING_REACH + block_offset + PAIR_BLOCK_COUNT])
    mirrored = jnp.stack(mirror_list, axis=1)
    gap_col = jnp.stack(gap_list, axis=1)
    denom = pair_gap[:, None, :, None] + gap_col[:, :, None, :]
    total = integral + cycle + mirrored
    new_amplitude = jnp.where(present[:, :, None, None] > 0, total / denom, jnp.float32(0.0))
    energy = jnp.sum(new_amplitude * integral) / (PAIRS_PER_BLOCK * PAIRS_PER_BLOCK * PAIR_BLOCK_COUNT)
    return new_amplitude, jnp.reshape(energy, (1,))
```

```python
import functools

import jax
import jax.numpy as jnp
from jax import lax
from jax.experimental import pallas as pl
from jax.experimental.pallas import tpu as pltpu
from jax.sharding import PartitionSpec as P

F32 = jnp.float32
EXTRA = 8


def own_slot(reach, offset, core):
    return reach + 2 * offset


def give_slot(reach, offset, core):
    return reach + 2 * offset + 1 - 2 * core


def twin_slot(reach, core):
    return reach + 1 - 2 * core


def far_slot(reach, core):
    return 2 * reach * core


def split(value):
    high = value.astype(jnp.bfloat16)
    low = (value - high.astype(F32)).astype(jnp.bfloat16)
    return high, low


def product(left, right, dims):
    def one(a, b):
        return lax.dot_general(a, b, (dims, ((), ())), preferred_element_type=F32)

    (left_high, left_low), (right_high, right_low) = left, right
    return one(left_high, right_high) + (one(left_high, right_low) + one(left_low, right_high))


def cycle_of(amp, integ):
    amp_parts = split(amp)
    inner = product(split(integ), amp_parts, ((1,), (1,)))
    inner = integ + integ.T - 0.5 * inner
    return product(amp_parts, split(inner), ((1,), (0,)))


def pick(index, options):
    value = options[-1]
    for place in range(len(options) - 2, -1, -1):
        value = jnp.where(index == place, options[place], value)
    return value


def give_kernel(core_ref, amp_ref, int_ref, gap_ref, out_ref):
    width = amp_ref.shape[-1]
    out_ref[0, :width, :] = cycle_of(amp_ref[0, 0], int_ref[0, 0])
    out_ref[0, width:, :] = jnp.broadcast_to(gap_ref[...], (EXTRA, width))


def bundle_kernel(paired, core_ref, amp_ref, int_ref, gap_ref, twin_ref, *outs):
    width = amp_ref.shape[-1]
    height = width + EXTRA
    step = pl.program_id(0)
    cycle = cycle_of(amp_ref[0, 0], int_ref[0, 0])
    for place, out_ref in enumerate(outs):

        @pl.when(step == place)
        def _():
            out_ref[:width, :] = cycle
            out_ref[width:height, :] = jnp.broadcast_to(gap_ref[...], (EXTRA, width))
            if paired[place]:
                out_ref[height:, :] = twin_ref[0]


def update(own, arrived, integ, gap_row, gap_other, flag):
    gap_column = jnp.broadcast_to(gap_row, (8, gap_row.shape[1])).T[:, :1]
    total = integ + own + arrived.T
    fresh = total / (gap_column + gap_other)
    return jnp.where(flag > 0, fresh, F32(0.0))


def fold(value):
    return jnp.sum(value.reshape(value.shape[0] // 8, 8, value.shape[1]), axis=0)


def first_kernel(core_ref, present_ref, amp_ref, int_ref, gap_ref, own_ref, arrived_ref, out_ref, part_ref):
    width = amp_ref.shape[-1]
    slots = present_ref.shape[1]
    reach = (slots - 1) // 2
    integ = int_ref[0, 0]
    step = pl.program_id(0)

    @pl.when(step == 0)
    def _():
        cycle = cycle_of(amp_ref[0, 0], integ)
        fresh = update(cycle, cycle, integ, gap_ref[...], gap_ref[...], present_ref[0, reach])
        out_ref[0, 0] = fresh
        part_ref[...] = fold(fresh * integ)

    @pl.when(step == 1)
    def _():
        flag = present_ref[0, twin_slot(reach, core_ref[0])]
        fresh = update(
            own_ref[0, :width], arrived_ref[0, :width], integ, gap_ref[...], arrived_ref[0, width : width + 1], flag
        )
        out_ref[0, 0] = fresh
        part_ref[...] += fold(fresh * integ)


def bundle_update_kernel(
    offset, core_ref, present_ref, int_ref, gap_ref, own_ref, given_ref, arrived_ref, before_ref, part_in_ref, out_ref, part_ref
):
    width = int_ref.shape[-1]
    reach = (present_ref.shape[1] - 1) // 2
    integ = int_ref[0, 0]
    step = pl.program_id(0)

    def one(own, slot, part):
        fresh = update(
            own, arrived_ref[:width], integ, gap_ref[...], arrived_ref[width : width + 1], present_ref[0, slot]
        )
        out_ref[0, 0] = fresh
        part_ref[...] = part + fold(fresh * integ)

    @pl.when(step == 0)
    def _():
        one(own_ref[:width], own_slot(reach, -offset, core_ref[0]), part_in_ref[...])

    @pl.when(step == 1)
    def _():
        one(given_ref[0, :width], give_slot(reach, -offset, core_ref[0]), part_ref[...])


def far_update_kernel(
    core_ref, present_ref, int_ref, gap_ref, own_ref, arrived_ref, before_ref, part_in_ref, out_ref, part_ref
):
    width = int_ref.shape[-1]
    reach = (present_ref.shape[1] - 1) // 2
    integ = int_ref[0, 0]
    fresh = update(
        own_ref[:width],
        arrived_ref[:width],
        integ,
        gap_ref[...],
        arrived_ref[width : width + 1],
        present_ref[0, far_slot(reach, core_ref[0])],
    )
    out_ref[0, 0] = fresh
    part_ref[...] = part_in_ref[...] + fold(fresh * integ)


def cost(blocks, width, products):
    return pl.CostEstimate(
        flops=blocks * products * 2 * width**3, bytes_accessed=blocks * 4 * 4 * width**2, transcendentals=0
    )


PARAMS = pltpu.CompilerParams(vmem_limit_bytes=32 * 1024 * 1024)


def per_device(amplitude, integral, pair_gap, present):
    slots, width = amplitude.shape[1], amplitude.shape[2]
    reach = (slots - 1) // 2
    height = width + EXTRA
    count = lax.axis_size("row")
    core = jnp.reshape(lax.rem(lax.axis_index("row"), 2), (1,)).astype(jnp.int32)

    def slot_spec(choose):
        return pl.BlockSpec((1, 1, width, width), lambda k, core_ref, *_: (0, choose(k, core_ref[0]), 0, 0))

    def whole(shape):
        return pl.BlockSpec(shape, lambda k, *_: (0,) * len(shape))

    gap_spec = whole((1, width))

    def shape(*dims):
        return jax.ShapeDtypeStruct(dims, F32)

    def gives(offsets, with_twin):
        def choose(k, c):
            options = [give_slot(reach, offset, c) for offset in offsets]
            return pick(k, options + ([twin_slot(reach, c)] if with_twin else []))

        blocks = len(offsets) + int(with_twin)
        return pl.pallas_call(
            give_kernel,
            grid_spec=pltpu.PrefetchScalarGridSpec(
                num_scalar_prefetch=1,
                grid=(blocks,),
                in_specs=[slot_spec(choose), slot_spec(choose), gap_spec],
                out_specs=pl.BlockSpec((1, height, width), lambda k, *_: (k, 0, 0)),
            ),
            out_shape=shape(blocks, height, width),
            compiler_params=PARAMS,
            cost_estimate=cost(blocks, width, 6),
            name="give_blocks",
        )(core, amplitude, integral, pair_gap)

    def bundles(offsets, with_far, swapped):
        def choose(k, c):
            options = [own_slot(reach, offset, c) for offset in offsets]
            return pick(k, options + ([far_slot(reach, c)] if with_far else []))

        paired = [True] * len(offsets) + [False] * int(with_far)
        heights = [2 * height if p else height for p in paired]
        return pl.pallas_call(
            functools.partial(bundle_kernel, paired),
            grid_spec=pltpu.PrefetchScalarGridSpec(
                num_scalar_prefetch=1,
                grid=(len(paired),),
                in_specs=[
                    slot_spec(choose),
                    slot_spec(choose),
                    gap_spec,
                    pl.BlockSpec((1, height, width), lambda k, *_: (jnp.minimum(k, len(offsets) - 1), 0, 0)),
                ],
                out_specs=[whole((h, width)) for h in heights],
            ),
            out_shape=[shape(h, width) for h in heights],
            compiler_params=PARAMS,
            cost_estimate=cost(len(paired), width, 6),
            name="bundles",
        )(core, amplitude, integral, pair_gap, swapped)

    def swap(value):
        return lax.ppermute(value, "row", [(place, place ^ 1) for place in range(count)])

    def along(value, steps):
        return lax.ppermute(
            value, "row", [(place, place + steps) for place in range(count) if 0 <= place + steps < count]
        )

    top = (reach - 1) // 2
    early = [2, -2]
    late = [3, -3, 1, -1]
    given_early = gives(early, False)
    swapped_early = swap(given_early)
    given_late = gives(late, True)
    swapped_late = swap(given_late)
    sent = dict(zip(early, bundles(early, False, swapped_early)))
    arrived = {offset: along(sent[offset], 2 * offset) for offset in early}
    *late_bundles, far = bundles(late, True, swapped_late)
    sent.update(zip(late, late_bundles))
    for offset in late:
        arrived[offset] = along(sent[offset], 2 * offset)
    far_pairs = [(place, place + reach) for place in range(1, count - reach, 2)]
    far_pairs += [(place, place - reach) for place in range(reach + 1, count, 2)]
    arrived_far = lax.ppermute(far, "row", far_pairs)
    given = {offset: (given_early, place) for place, offset in enumerate(early)}
    given.update({offset: (given_late, place) for place, offset in enumerate(late)})

    out_shape = [shape(1, slots, width, width), shape(8, width)]
    twin_place = len(late)
    twin_block = pl.BlockSpec((1, height, width), lambda k, *_: (twin_place, 0, 0))

    def first_choose(k, c):
        return jnp.where(k == 0, reach, twin_slot(reach, c))

    updated, part = pl.pallas_call(
        first_kernel,
        grid_spec=pltpu.PrefetchScalarGridSpec(
            num_scalar_prefetch=2,
            grid=(2,),
            in_specs=[
                slot_spec(lambda k, c: reach),
                slot_spec(first_choose),
                gap_spec,
                twin_block,
                twin_block,
            ],
            out_specs=[slot_spec(first_choose), whole((8, width))],
        ),
        out_shape=out_shape,
        compiler_params=PARAMS,
        cost_estimate=cost(2, width, 3),
        name="first_update",
    )(core, present, amplitude, integral, pair_gap, given_late, swapped_late)

    def bundle_update(offset, updated, part):
        source, place = given[-offset]

        def choose(k, c):
            return jnp.where(k == 0, own_slot(reach, -offset, c), give_slot(reach, -offset, c))

        return pl.pallas_call(
            functools.partial(bundle_update_kernel, offset),
            grid_spec=pltpu.PrefetchScalarGridSpec(
                num_scalar_prefetch=2,
                grid=(2,),
                in_specs=[
                    slot_spec(choose),
                    gap_spec,
                    whole((height, width)),
                    pl.BlockSpec((1, height, width), lambda k, *_: (place, 0, 0)),
                    pl.BlockSpec((height, width), lambda k, *_: (k, 0)),
                    pl.BlockSpec(memory_space=pl.ANY),
                    whole((8, width)),
                ],
                out_specs=[slot_spec(choose), whole((8, width))],
            ),
            out_shape=out_shape,
            input_output_aliases={7: 0},
            compiler_params=PARAMS,
            cost_estimate=cost(2, width, 0),
            name="bundle_update",
        )(core, present, integral, pair_gap, sent[-offset], source, arrived[offset], updated, part)

    for offset in early + late:
        updated, part = bundle_update(offset, updated, part)

    far_choose = lambda k, c: far_slot(reach, c)
    updated, part = pl.pallas_call(
        far_update_kernel,
        grid_spec=pltpu.PrefetchScalarGridSpec(
            num_scalar_prefetch=2,
            grid=(1,),
            in_specs=[
                slot_spec(far_choose),
                gap_spec,
                whole((height, width)),
                whole((height, width)),
                pl.BlockSpec(memory_space=pl.ANY),
                whole((8, width)),
            ],
            out_specs=[slot_spec(far_choose), whole((8, width))],
        ),
        out_shape=out_shape,
        input_output_aliases={6: 0},
        compiler_params=PARAMS,
        cost_estimate=cost(1, width, 0),
        name="far_update",
    )(core, present, integral, pair_gap, far, arrived_far, updated, part)

    summed = jnp.sum(part, axis=0).reshape(-1, 128).sum(axis=0)
    every = lax.all_to_all(jnp.broadcast_to(summed, (count, 128)), "row", 0, 0)
    blocks_all = count * amplitude.shape[0]
    energy = jnp.sum(every) / (width * width * blocks_all)
    return updated, jnp.reshape(energy, (1,))


def solution(mesh):
    in_specs = (
        P(("mol", "row"), None, None, None),
        P(("mol", "row"), None, None, None),
        P(("mol", "row"), None),
        P(("mol", "row"), None),
    )
    out_specs = (P(("mol", "row"), None, None, None), P("mol"))
    return jax.shard_map(per_device, mesh=mesh, in_specs=in_specs, out_specs=out_specs, check_vma=False)
```

```python
import functools

import jax
import jax.numpy as jnp
from jax import lax
from jax.experimental import pallas as pl
from jax.experimental.pallas import tpu as pltpu
from jax.sharding import PartitionSpec as P

F32 = jnp.float32
EXTRA = 8

SENDS = (
    (2, 7, -1, 6, 1, 10, 13, 3, 14, 8, 9, 4, 5, 12, 15, 11),
    (6, 0, 7, -1, 11, 3, 9, 2, 13, 4, 5, 12, -1, 8, -1, 10),
    (7, -1, 3, 10, 5, 12, -1, 1, 9, 2, 4, 13, -1, 11, -1, 8),
    (-1, 6, -1, -1, -1, 9, 11, 4, 10, 3, 13, -1, 8, -1, 7, -1),
    (-1, 8, -1, 7, 6, 4, 2, 12, 3, 10, 11, 5, -1, -1, -1, 9),
    (1, 4, 5, -1, 3, 8, 0, 9, 12, 7, 14, 6, 10, 15, 11, 13),
    (-1, 5, 6, 2, 9, 1, 7, 8, 4, 11, 3, -1, 15, -1, 13, 14),
    (5, -1, -1, 4, -1, 11, 10, 6, 2, 14, 12, 7, 9, -1, 8, -1),
    (4, 3, -1, 5, 8, -1, 12, 0, 11, 6, 7, -1, 14, -1, 9, -1),
    (-1, 2, -1, 0, 10, 7, 8, 5, 1, -1, -1, 15, -1, 9, 12, -1),
    (-1, -1, 0, -1, 2, 6, 4, 10, 5, 13, 15, 8, 11, -1, -1, -1),
    (-1, -1, 4, 1, 0, -1, 3, 13, 6, 12, 8, 10, -1, 14, -1, -1),
    (3, -1, -1, -1, 7, 0, 1, 14, 15, 5, 6, 9, -1, -1, 10, 12),
    (-1, -1, 1, -1, -1, 2, 5, 11, 7, 15, -1, 14, 13, 10, -1, -1),
)
RELAYS = (
    (2, 0, 9, 0, 10),
    (3, 1, 9, 1, 11),
    (12, 14, 7, 1, 11),
    (12, 14, 6, 2, 13),
    (3, 1, 8, 3, 12),
    (13, 15, 6, 3, 9),
    (2, 0, 8, 4, 13),
    (13, 15, 7, 4, 10),
)


def rounds_of(count, reach):
    rounds = []
    if count != len(SENDS[0]):
        for step in range(reach, 0, -1):
            for offset in (step, -step):
                pairs = [(row, row + offset) for row in range(count) if 0 <= row + offset < count]
                rounds.append((pairs, [reach + offset] * count, [reach - offset] * count))
        return rounds, ()
    for number, targets in enumerate(SENDS):
        pairs, sent, received = [], [None] * count, [None] * count
        for row, target in enumerate(targets):
            if target >= 0:
                pairs.append((row, target))
                sent[row], received[target] = reach + target - row, reach + row - target
        for origin, by, to, first, second in RELAYS:
            if number == first:
                pairs.append((origin, by))
                sent[origin] = reach + to - origin
            if number == second:
                pairs.append((by, to))
                received[to] = reach + origin - to
        rounds.append((pairs, sent, received))
    for row in range(count):
        for kind in (1, 2):
            used = {turn[kind][row] for turn in rounds}
            spare = [slot for slot in range(2 * reach + 1) if slot != reach and slot not in used]
            for turn in rounds:
                if turn[kind][row] is None:
                    turn[kind][row] = spare.pop()
    return rounds, RELAYS


def lookup(values, here):
    if len(set(values)) == 1:
        return values[0]
    words = [sum(value << 4 * place for place, value in enumerate(values[at : at + 8])) for at in (0, 8)]
    low, high = [word - 2**32 if word >= 2**31 else word for word in words]
    word = jnp.where(here < 8, jnp.int32(low), jnp.int32(high))
    return lax.shift_right_logical(word, 4 * lax.rem(here, 8)) & 15


def split(value):
    high = value.astype(jnp.bfloat16)
    low = (value - high.astype(F32)).astype(jnp.bfloat16)
    return high, low


def product(left, right):
    def one(a, b):
        return jnp.dot(a, b, preferred_element_type=F32)

    (left_high, left_low), (right_high, right_low) = left, right
    return one(left_high, right_high) + (one(left_high, right_low) + one(left_low, right_high))


def cycle_of(amp, integ):
    inner = product(split(integ), split(amp.T))
    inner = integ + integ.T - 0.5 * inner
    return product(split(amp), split(inner))


def put_cycles(slots, here, amp_ref, int_ref, gap_rows, kept_ref, outs):
    width = amp_ref.shape[-1]
    for number, slot in enumerate(slots):
        index = lookup(slot, here)
        cycle = cycle_of(amp_ref[index], int_ref[index])
        kept_ref[index] = cycle
        if number < len(outs):
            outs[number][:width, :] = cycle
            outs[number][width:, :] = gap_rows


def first_kernel(order, amp_hbm, int_hbm, gap_hbm, present_hbm, *refs):
    amp_ref, int_ref, gap_ref, present_ref, kept_ref, *outs = refs[:-3]
    gap_buf, block_sem, small_sem = refs[-3:]
    here = lax.axis_index("row")
    loads = []
    for number, slot in enumerate(order):
        index = lookup(slot, here)
        loads.append(pltpu.make_async_copy(amp_hbm.at[0, index], amp_ref.at[index], block_sem.at[number, 0]))
        loads.append(pltpu.make_async_copy(int_hbm.at[0, index], int_ref.at[index], block_sem.at[number, 1]))
        loads[-2].start()
        loads[-1].start()
        if number == 0:
            small = [
                pltpu.make_async_copy(gap_hbm, gap_buf, small_sem.at[0]),
                pltpu.make_async_copy(present_hbm, present_ref, small_sem.at[1]),
            ]
            for copy in small:
                copy.start()
    for copy in loads[: 2 * len(outs)] + small:
        copy.wait()
    gap_rows = jnp.broadcast_to(gap_buf[...], (EXTRA, amp_ref.shape[-1]))
    gap_ref[...] = gap_rows
    put_cycles(order[: len(outs)], here, amp_ref, int_ref, gap_rows, kept_ref, outs)
    for copy in loads[2 * len(outs) :]:
        copy.wait()


def cycle_kernel(order, relays, arrays, amp_ref, int_ref, gap_ref, _, *refs):
    arrived, kept_ref, outs = refs[:arrays], refs[arrays], refs[arrays + 1 :]
    here = lax.axis_index("row")
    put_cycles(order, here, amp_ref, int_ref, gap_ref[...], kept_ref, outs)
    for row, output, array in relays:

        @pl.when(here == row)
        def _():
            outs[output][...] = arrived[array][...]


def update_kernel(slots, first, int_ref, gap_ref, present_ref, kept_ref, *refs):
    arrived, refs = refs[: len(slots)], refs[len(slots) :]
    if not first:
        before_ref, refs = refs[1], refs[2:]
    out_ref, part_ref, out_buf, out_sem = refs
    width = int_ref.shape[-1]
    middle = (present_ref.shape[1] - 1) // 2
    here = lax.axis_index("row")
    gap_column = gap_ref[...].T[:, :1]
    part = jnp.zeros(part_ref.shape, F32) if first else before_ref[...]
    stores = []
    items = [(lookup(slot, here), ref) for slot, ref in zip(slots, arrived)]
    if first:
        items.append((middle, None))
    for number, (index, ref) in enumerate(items):
        integ, mine = int_ref[index], kept_ref[index]
        theirs = mine if ref is None else ref[:width, :]
        gap_other = gap_ref[:1, :] if ref is None else ref[width : width + 1, :]
        at_slot = lax.broadcasted_iota(jnp.int32, present_ref.shape, 1) == index
        flag = jnp.sum(jnp.where(at_slot, present_ref[...], 0), axis=1, keepdims=True)
        total = integ + mine + theirs.T
        fresh = jnp.where(flag > 0, total / (gap_column + gap_other), F32(0.0))
        out_buf[number] = fresh
        stores.append(pltpu.make_async_copy(out_buf.at[number], out_ref.at[0, index], out_sem.at[number]))
        stores[-1].start()
        part = part + jnp.sum((fresh * integ).reshape(width // 8, 8, width), axis=0)
    part_ref[...] = part
    for copy in stores:
        copy.wait()


PARAMS = pltpu.CompilerParams(vmem_limit_bytes=16 * 1024 * 1024)
IN_HBM = pl.BlockSpec(memory_space=pltpu.HBM)
IN_VMEM = pl.BlockSpec(memory_space=pltpu.VMEM)
DMA = pltpu.SemaphoreType.DMA
SMALL = pl.CostEstimate(flops=1, bytes_accessed=1, transcendentals=0)
FIRST, SECOND = 4, 8
UPDATES = (0, 5, 10, 14)


def per_device(amplitude, integral, pair_gap, present):
    slots, width = amplitude.shape[1], amplitude.shape[2]
    reach = (slots - 1) // 2
    height = width + EXTRA
    count = lax.axis_size("row")
    rounds, relays = rounds_of(count, reach)
    order = [turn[1] for turn in rounds] + [[reach]]

    def hbm(*values):
        return [pltpu.with_memory_space_constraint(value, pltpu.HBM) for value in values]

    def vmem(*values):
        return [pltpu.with_memory_space_constraint(value, pltpu.VMEM) for value in values]

    cube = pltpu.VMEM((slots, width, width), F32)
    block = pltpu.VMEM((height, width), F32)
    amp, integ, gap, flags, kept, *sent = pl.pallas_call(
        functools.partial(first_kernel, order),
        in_specs=[IN_HBM] * 4,
        out_specs=[IN_VMEM] * (5 + FIRST),
        out_shape=[cube, cube, pltpu.VMEM((EXTRA, width), F32), pltpu.VMEM(present.shape, present.dtype), cube]
        + [block] * FIRST,
        scratch_shapes=[pltpu.VMEM((1, width), F32), DMA((slots, 2)), DMA((2,))],
        compiler_params=PARAMS,
        cost_estimate=SMALL,
        name="first_blocks",
    )(*hbm(amplitude, integral, pair_gap, present))

    def cycles(name, start, stop, kept, arrived):
        passed = [(by, second - start, first) for _, by, _, first, second in relays if start <= second < stop]
        arrived = arrived if passed else []
        some = order[start:stop] + ([order[-1]] if stop == len(rounds) else [])
        kept, *sent = pl.pallas_call(
            functools.partial(cycle_kernel, some, passed, len(arrived)),
            in_specs=[IN_VMEM] * (4 + len(arrived)),
            out_specs=[IN_VMEM] * (1 + stop - start),
            out_shape=[cube] + [block] * (stop - start),
            input_output_aliases={3: 0},
            compiler_params=PARAMS,
            cost_estimate=SMALL,
            name=name,
        )(*vmem(amp, integ, gap, kept, *arrived))
        return kept, sent

    def send(start, stop):
        return [lax.ppermute(sent[number], "row", rounds[number][0]) for number in range(start, stop)]

    arrived = send(0, FIRST)
    kept, more = cycles("second_blocks", FIRST, SECOND, kept, [])
    sent += more
    arrived += send(FIRST, SECOND)
    passing = 1 + max([first for _, _, _, first, _ in relays], default=-1)
    kept, more = cycles("third_blocks", SECOND, len(rounds), kept, arrived[:passing])
    sent += more
    arrived += send(SECOND, len(rounds))

    def updates(start, stop, before):
        some = [turn[2] for turn in rounds[start:stop]]
        first = before is None
        n = len(some) + int(first)
        return pl.pallas_call(
            functools.partial(update_kernel, some, first),
            in_specs=[IN_VMEM] * (4 + len(some)) + ([] if first else [IN_HBM, IN_VMEM]),
            out_specs=[IN_HBM, IN_VMEM],
            out_shape=[pltpu.HBM((1, slots, width, width), F32), pltpu.VMEM((8, width), F32)],
            scratch_shapes=[pltpu.VMEM((n, width, width), F32), DMA((n,))],
            input_output_aliases={} if first else {4 + len(some): 0},
            compiler_params=PARAMS,
            cost_estimate=SMALL,
            name="update",
        )(
            *vmem(integ, gap, flags, kept, *arrived[start:stop]),
            *([] if first else [*hbm(before[0]), *vmem(before[1])]),
        )

    state = None
    for start, stop in zip(UPDATES[:-1], UPDATES[1:]):
        state = updates(start, stop, state)
    updated, part = state

    summed = jnp.sum(part, axis=0).reshape(-1, 128).sum(axis=0)
    every = lax.all_to_all(jnp.broadcast_to(summed, (count, 128)), "row", 0, 0)
    blocks_all = count * amplitude.shape[0]
    energy = jnp.sum(every) / (width * width * blocks_all)
    return updated, jnp.reshape(energy, (1,))


def solution(mesh):
    in_specs = (
        P(("mol", "row"), None, None, None),
        P(("mol", "row"), None, None, None),
        P(("mol", "row"), None),
        P(("mol", "row"), None),
    )
    out_specs = (P(("mol", "row"), None, None, None), P("mol"))
    return jax.shard_map(per_device, mesh=mesh, in_specs=in_specs, out_specs=out_specs, check_vma=False)
```

```python
import functools

import jax
import jax.numpy as jnp
from jax import lax
from jax.experimental import pallas as pl
from jax.experimental.pallas import tpu as pltpu
from jax.sharding import PartitionSpec as P

F32 = jnp.float32
EXTRA = 8

SENDS = (
    (2, 7, 6, -1, 16, 12, 3, 9, 10, 8, 14, 4, 5, -1, 13, 11),
    (17, 8, -1, 7, 2, 4, 10, 5, 6, 12, 3, 15, -1, 11, 9, 29),
    (4, 0, 19, -1, 11, 2, 7, 13, 9, 6, 5, 10, -1, 28, 31, 8),
    (18, 6, -1, 5, 8, 1, 9, 3, 4, 11, 7, 14, 29, -1, 10, 28),
    (19, 4, 7, 18, 22, 8, 12, 0, 1, 10, 9, 5, 29, 31, 27, 30),
    (17, 5, 0, 18, 9, 7, 13, 6, 3, 15, 4, 26, 11, 12, 8, 30),
    (7, 16, 17, 18, 21, 9, 8, 4, 11, 3, 12, 6, 29, 30, 15, 10),
    (6, 3, 5, 1, 10, 0, 11, 2, 12, 4, 13, 9, 8, 15, 7, 30),
    (1, -1, 19, 0, 5, 6, 4, 8, 14, 2, 27, 13, 10, 28, 31, -1),
    (-1, 2, 19, 10, 0, 20, 5, 1, 15, 7, 6, 12, 29, 25, 11, 14),
    (17, 21, 4, 2, 3, 11, 0, 10, 7, 13, 8, 31, 14, 9, 12, -1),
    (3, -1, 16, 6, 1, 20, 2, 11, 5, 28, 15, 26, 9, 14, -1, 13),
    (5, 16, 3, 4, 6, 10, 1, 12, 2, 14, 11, 7, 13, 8, 31, 9),
    (-1, 16, 1, 18, 7, 3, 20, 14, 13, 5, 27, 8, 15, 10, -1, 12),
)
RELAYS = (
    (3, 1, 8, 0, 11),
    (13, 15, 6, 0, 10),
    (2, 0, 8, 1, 9),
    (12, 14, 6, 1, 13),
    (3, 1, 9, 2, 8),
    (12, 14, 7, 2, 11),
    (2, 0, 9, 3, 13),
    (13, 15, 7, 3, 8),
)


def rounds_of(count, reach):
    rounds = []
    if count != len(SENDS[0]):
        for step in range(reach, 0, -1):
            for offset in (step, -step):
                pairs = [(row, (row + offset) % count) for row in range(count)]
                rounds.append((pairs, [reach + offset] * count, [reach - offset] * count))
        return rounds, ()
    for number, targets in enumerate(SENDS):
        pairs, sent, received = [], [None] * count, [None] * count
        for row, target in enumerate(targets):
            if target >= 0:
                pairs.append((row, target % count))
            if 0 <= target < count:
                sent[row], received[target] = reach + target - row, reach + row - target
        for origin, by, to, first, second in RELAYS:
            if number == first:
                pairs.append((origin, by))
                sent[origin] = reach + to - origin
            if number == second:
                pairs.append((by, to))
                received[to] = reach + origin - to
        rounds.append((pairs, sent, received))
    for row in range(count):
        for kind in (1, 2):
            used = {turn[kind][row] for turn in rounds}
            spare = [slot for slot in range(2 * reach + 1) if slot != reach and slot not in used]
            for turn in rounds:
                if turn[kind][row] is None:
                    turn[kind][row] = spare.pop()
    return rounds, RELAYS


def lookup(values, here):
    if len(set(values)) == 1:
        return values[0]
    words = [sum(value << 4 * place for place, value in enumerate(values[at : at + 8])) for at in (0, 8)]
    low, high = [word - 2**32 if word >= 2**31 else word for word in words]
    word = jnp.where(here < 8, jnp.int32(low), jnp.int32(high))
    return lax.shift_right_logical(word, 4 * lax.rem(here, 8)) & 15


def split(value):
    high = value.astype(jnp.bfloat16)
    low = (value - high.astype(F32)).astype(jnp.bfloat16)
    return high, low


def product(left, right):
    def one(a, b):
        return jnp.dot(a, b, preferred_element_type=F32)

    (left_high, left_low), (right_high, right_low) = left, right
    return one(left_high, right_high) + (one(left_high, right_low) + one(left_low, right_high))


def cycle_of(amp, integ):
    inner = product(split(integ), split(amp.T))
    inner = integ + integ.T - 0.5 * inner
    return product(split(amp), split(inner))


def put_cycle(amp, integ, gap_rows, kept_ref, out_ref):
    cycle = cycle_of(amp, integ)
    kept_ref[...] = cycle
    if out_ref is not None:
        out_ref[: cycle.shape[0], :] = cycle
        out_ref[cycle.shape[0] :, :] = gap_rows


def first_kernel(order, amp_hbm, int_hbm, gap_hbm, present_hbm, *refs):
    gap_ref, present_ref, kept_ref, *outs = refs[:-5]
    amp_buf, int_buf, gap_buf, block_sem, small_sem = refs[-5:]
    here = lax.axis_index("row")
    places = [lookup(slot, here) for slot in order]
    loads = []
    for number, index in enumerate(places):
        loads.append(pltpu.make_async_copy(amp_hbm.at[0, index], amp_buf.at[number], block_sem.at[number, 0]))
        loads.append(pltpu.make_async_copy(int_hbm.at[0, index], int_buf.at[number], block_sem.at[number, 1]))
        loads[-2].start()
        loads[-1].start()
    loads.append(pltpu.make_async_copy(gap_hbm, gap_buf, small_sem.at[0]))
    loads.append(pltpu.make_async_copy(present_hbm, present_ref, small_sem.at[1]))
    loads[-2].start()
    loads[-1].start()
    for copy in loads:
        copy.wait()
    gap_rows = jnp.broadcast_to(gap_buf[...], (EXTRA, amp_buf.shape[-1]))
    gap_ref[...] = gap_rows
    for number, index in enumerate(places):
        put_cycle(amp_buf[number], int_buf[number], gap_rows, kept_ref.at[index], outs[number])


def cycle_kernel(order, relays, arrays, amp_ref, int_ref, gap_ref, _, *refs):
    arrived, kept_ref, outs = refs[:arrays], refs[arrays], refs[arrays + 1 :]
    here = lax.axis_index("row")
    for slot, out_ref in zip(order, [*outs, None]):
        index = lookup(slot, here)
        put_cycle(amp_ref[0, index], int_ref[0, index], gap_ref[...], kept_ref.at[index], out_ref)
    for row, output, array in relays:

        @pl.when(here == row)
        def _():
            outs[output][...] = arrived[array][...]


def update_kernel(slots, first, int_ref, gap_ref, present_ref, kept_ref, *refs):
    arrived, refs = refs[: len(slots)], refs[len(slots) :]
    if not first:
        before_ref, refs = refs[1], refs[2:]
    out_ref, part_ref, out_buf, out_sem = refs
    width = int_ref.shape[-1]
    middle = (present_ref.shape[1] - 1) // 2
    here = lax.axis_index("row")
    gap_column = gap_ref[...].T[:, :1]
    part = jnp.zeros(part_ref.shape, F32) if first else before_ref[...]
    stores = []
    items = [(lookup(slot, here), ref) for slot, ref in zip(slots, arrived)]
    if first:
        items.append((middle, None))
    for number, (index, ref) in enumerate(items):
        integ, mine = int_ref[0, index], kept_ref[index]
        theirs = mine if ref is None else ref[:width, :]
        gap_other = gap_ref[:1, :] if ref is None else ref[width : width + 1, :]
        at_slot = lax.broadcasted_iota(jnp.int32, present_ref.shape, 1) == index
        flag = jnp.sum(jnp.where(at_slot, present_ref[...], 0), axis=1, keepdims=True)
        total = integ + mine + theirs.T
        fresh = jnp.where(flag > 0, total / (gap_column + gap_other), F32(0.0))
        out_buf[number] = fresh
        stores.append(pltpu.make_async_copy(out_buf.at[number], out_ref.at[0, index], out_sem.at[number]))
        stores[-1].start()
        part = part + jnp.sum((fresh * integ).reshape(width // 8, 8, width), axis=0)
    part_ref[...] = part
    for copy in stores:
        copy.wait()


PARAMS = pltpu.CompilerParams(vmem_limit_bytes=16 * 1024 * 1024)
IN_HBM = pl.BlockSpec(memory_space=pltpu.HBM)
IN_VMEM = pl.BlockSpec(memory_space=pltpu.VMEM)
DMA = pltpu.SemaphoreType.DMA
SMALL = pl.CostEstimate(flops=1, bytes_accessed=1, transcendentals=0)
FIRST, SECOND = 4, 8
UPDATES = (0, 5, 10, 14)


def per_device(amplitude, integral, pair_gap, present):
    slots, width = amplitude.shape[1], amplitude.shape[2]
    reach = (slots - 1) // 2
    height = width + EXTRA
    count = lax.axis_size("row")
    rounds, relays = rounds_of(count, reach)
    order = [turn[1] for turn in rounds] + [[reach]]

    def hbm(*values):
        return [pltpu.with_memory_space_constraint(value, pltpu.HBM) for value in values]

    def vmem(*values):
        return [pltpu.with_memory_space_constraint(value, pltpu.VMEM) for value in values]

    cube = pltpu.VMEM((slots, width, width), F32)
    block = pltpu.VMEM((height, width), F32)
    gap, flags, kept, *sent = pl.pallas_call(
        functools.partial(first_kernel, order[:FIRST]),
        in_specs=[IN_HBM] * 4,
        out_specs=[IN_VMEM] * (3 + FIRST),
        out_shape=[pltpu.VMEM((EXTRA, width), F32), pltpu.VMEM(present.shape, present.dtype), cube]
        + [block] * FIRST,
        scratch_shapes=[
            pltpu.VMEM((FIRST, width, width), F32),
            pltpu.VMEM((FIRST, width, width), F32),
            pltpu.VMEM((1, width), F32),
            DMA((FIRST, 2)),
            DMA((2,)),
        ],
        compiler_params=PARAMS,
        cost_estimate=SMALL,
        name="first_blocks",
    )(*hbm(amplitude, integral, pair_gap, present))

    def cycles(name, start, stop, kept, arrived):
        passed = [(by, second - start, first) for _, by, _, first, second in relays if start <= second < stop]
        arrived = arrived if passed else []
        some = order[start:stop] + ([order[-1]] if stop == len(rounds) else [])
        kept, *sent = pl.pallas_call(
            functools.partial(cycle_kernel, some, passed, len(arrived)),
            in_specs=[IN_VMEM] * (4 + len(arrived)),
            out_specs=[IN_VMEM] * (1 + stop - start),
            out_shape=[cube] + [block] * (stop - start),
            input_output_aliases={3: 0},
            compiler_params=PARAMS,
            cost_estimate=SMALL,
            name=name,
        )(*vmem(amplitude, integral, gap, kept, *arrived))
        return kept, sent

    def send(start, stop):
        return [lax.ppermute(sent[number], "row", rounds[number][0]) for number in range(start, stop)]

    arrived = send(0, FIRST)
    kept, more = cycles("second_blocks", FIRST, SECOND, kept, [])
    sent += more
    arrived += send(FIRST, SECOND)
    passing = 1 + max([first for _, _, _, first, _ in relays], default=-1)
    kept, more = cycles("third_blocks", SECOND, len(rounds), kept, arrived[:passing])
    sent += more
    arrived += send(SECOND, len(rounds))

    def updates(start, stop, before):
        some = [turn[2] for turn in rounds[start:stop]]
        first = before is None
        n = len(some) + int(first)
        return pl.pallas_call(
            functools.partial(update_kernel, some, first),
            in_specs=[IN_VMEM] * (4 + len(some)) + ([] if first else [IN_HBM, IN_VMEM]),
            out_specs=[IN_HBM, IN_VMEM],
            out_shape=[pltpu.HBM((1, slots, width, width), F32), pltpu.VMEM((8, width), F32)],
            scratch_shapes=[pltpu.VMEM((n, width, width), F32), DMA((n,))],
            input_output_aliases={} if first else {4 + len(some): 0},
            compiler_params=PARAMS,
            cost_estimate=SMALL,
            name="update",
        )(
            *vmem(integral, gap, flags, kept, *arrived[start:stop]),
            *([] if first else [*hbm(before[0]), *vmem(before[1])]),
        )

    state = None
    for start, stop in zip(UPDATES[:-1], UPDATES[1:]):
        state = updates(start, stop, state)
    updated, part = state

    summed = jnp.sum(part, axis=0).reshape(-1, 128).sum(axis=0)
    every = lax.all_to_all(jnp.broadcast_to(summed, (count, 128)), "row", 0, 0)
    blocks_all = count * amplitude.shape[0]
    energy = jnp.sum(every) / (width * width * blocks_all)
    return updated, jnp.reshape(energy, (1,))


def solution(mesh):
    in_specs = (
        P(("mol", "row"), None, None, None),
        P(("mol", "row"), None, None, None),
        P(("mol", "row"), None),
        P(("mol", "row"), None),
    )
    out_specs = (P(("mol", "row"), None, None, None), P("mol"))
    return jax.shard_map(per_device, mesh=mesh, in_specs=in_specs, out_specs=out_specs, check_vma=False)
```

```python
import functools

import jax
import jax.numpy as jnp
from jax import lax
from jax.experimental import pallas as pl
from jax.experimental.pallas import tpu as pltpu
from jax.sharding import PartitionSpec as P

F32 = jnp.float32
EXTRA = 8
HALF = 128

SENDS = (
    (3, 5, -1, 6, 1, 8, 11, 2, 7, 13, 4, 14, 10, -1, 9, 12),
    (17, 8, -1, 7, 3, 6, 18, 9, 5, 10, 14, 4, 29, -1, 27, 28),
    (18, 6, 5, -1, 11, 0, 10, 3, 4, 8, 7, 31, -1, 28, 13, 9),
    (5, 0, 3, -1, 8, 7, 13, 4, 2, 12, 9, 6, -1, 10, 15, 11),
    (2, 7, 19, 0, 17, 10, 8, 6, 9, 4, 5, 15, 14, 28, 11, 13),
    (18, 4, 6, 16, 21, 12, 3, 10, 1, 11, 13, 8, 31, 9, 7, 30),
    (6, 3, 4, 18, 10, 1, 0, 14, 12, 5, 27, 7, 9, 31, 29, 8),
    (4, 16, 17, 18, 9, 3, 7, 13, 14, 6, 27, 5, 8, 28, 31, 10),
    (20, 16, 1, 10, 7, 9, 2, 5, 13, 3, 6, 12, 11, 15, 8, 30),
    (1, -1, 7, 2, 5, 4, 9, 0, 3, 14, 15, 26, 29, 11, 12, -1),
    (7, 16, 19, 1, 21, 11, 4, 12, 15, 2, 8, 10, 13, 25, -1, 14),
    (17, -1, 0, 22, 2, 20, 5, 8, 11, 7, 3, 13, 15, 12, 10, 30),
    (-1, 2, 19, 5, 0, 20, 1, 11, 6, 15, 12, 26, 29, 8, -1, 30),
    (-1, 16, 19, 4, 6, 2, 12, 1, 10, 29, 11, 9, 5, 14, 31, -1),
)
RELAYS = (
    (2, 0, 9, 0, 12),
    (13, 15, 6, 0, 9),
    (2, 0, 8, 1, 13),
    (13, 15, 7, 1, 13),
    (3, 1, 8, 2, 9),
    (12, 14, 7, 2, 12),
    (3, 1, 9, 3, 11),
    (12, 14, 6, 3, 10),
)


def rounds_of(count, reach):
    rounds = []
    if count != len(SENDS[0]):
        for step in range(reach, 0, -1):
            for offset in (step, -step):
                pairs = [(row, (row + offset) % count) for row in range(count)]
                rounds.append((pairs, [reach + offset] * count, [reach - offset] * count))
        return rounds, ()
    for number, targets in enumerate(SENDS):
        pairs, sent, received = [], [None] * count, [None] * count
        for row, target in enumerate(targets):
            if target >= 0:
                pairs.append((row, target % count))
            if 0 <= target < count:
                sent[row], received[target] = reach + target - row, reach + row - target
        for origin, by, to, first, second in RELAYS:
            if number == first:
                pairs.append((origin, by))
                sent[origin] = reach + to - origin
            if number == second:
                pairs.append((by, to))
                received[to] = reach + origin - to
        rounds.append((pairs, sent, received))
    for row in range(count):
        for kind in (1, 2):
            used = {turn[kind][row] for turn in rounds}
            spare = [slot for slot in range(2 * reach + 1) if slot != reach and slot not in used]
            for turn in rounds:
                if turn[kind][row] is None:
                    turn[kind][row] = spare.pop()
    return rounds, RELAYS


def lookup(values, here):
    if len(set(values)) == 1:
        return values[0]
    words = [sum(value << 4 * place for place, value in enumerate(values[at : at + 8])) for at in (0, 8)]
    low, high = [word - 2**32 if word >= 2**31 else word for word in words]
    word = jnp.where(here < 8, jnp.int32(low), jnp.int32(high))
    return lax.shift_right_logical(word, 4 * lax.rem(here, 8)) & 15


def split(value):
    high = value.astype(jnp.bfloat16)
    low = (value - high.astype(F32)).astype(jnp.bfloat16)
    return high, low


def product(left, right):
    def one(a, b):
        return jnp.dot(a, b, preferred_element_type=F32)

    (left_high, left_low), (right_high, right_low) = left, right
    return one(left_high, right_high) + (one(left_high, right_low) + one(left_low, right_high))


def cycle_of(amp, integ):
    inner = product(split(integ), split(amp.T))
    inner = integ + integ.T - 0.5 * inner
    return product(split(amp), split(inner))


def halves(value):
    return [value[:, :HALF], value[:, HALF:]]


def put_cycle(amp, integ, gap_row, kept_ref, out_ref):
    cycle = cycle_of(amp, integ)
    kept_ref[...] = cycle
    if out_ref is not None:
        height = cycle.shape[0]
        for side, part in enumerate(halves(cycle)):
            out_ref[pl.ds(side * height, height), :] = part
        out_ref[pl.ds(2 * height, EXTRA), :] = jnp.concatenate(halves(gap_row) * (EXTRA // 2), axis=0)


def first_kernel(order, amp_hbm, int_hbm, gap_hbm, present_hbm, *refs):
    gap_ref, present_ref, kept_ref, *outs = refs[:-5]
    amp_buf, int_buf, gap_buf, block_sem, small_sem = refs[-5:]
    here = lax.axis_index("row")
    places = [lookup(slot, here) for slot in order]
    loads = []
    for number, index in enumerate(places):
        loads.append(pltpu.make_async_copy(amp_hbm.at[0, index], amp_buf.at[number], block_sem.at[number, 0]))
        loads.append(pltpu.make_async_copy(int_hbm.at[0, index], int_buf.at[number], block_sem.at[number, 1]))
        loads[-2].start()
        loads[-1].start()
    loads.append(pltpu.make_async_copy(gap_hbm, gap_buf, small_sem.at[0]))
    loads.append(pltpu.make_async_copy(present_hbm, present_ref, small_sem.at[1]))
    loads[-2].start()
    loads[-1].start()
    for copy in loads:
        copy.wait()
    gap_ref[...] = jnp.broadcast_to(gap_buf[...], gap_ref.shape)
    for number, index in enumerate(places):
        put_cycle(amp_buf[number], int_buf[number], gap_buf[...], kept_ref.at[index], outs[number])


def cycle_kernel(order, relays, arrays, amp_ref, int_ref, gap_ref, _, *refs):
    arrived, kept_ref, outs = refs[:arrays], refs[arrays], refs[arrays + 1 :]
    here = lax.axis_index("row")
    for slot, out_ref in zip(order, [*outs, None]):
        index = lookup(slot, here)
        put_cycle(amp_ref[0, index], int_ref[0, index], gap_ref[:1, :], kept_ref.at[index], out_ref)
    for row, output, array in relays:

        @pl.when(here == row)
        def _():
            outs[output][...] = arrived[array][...]


def update_kernel(slots, first, held, int_ref, gap_ref, present_ref, kept_ref, *refs):
    arrived, refs = refs[: len(slots)], refs[len(slots) :]
    if not first:
        before_ref, refs = refs[-3 - 2 * (not held)], refs[-2 - 2 * (not held) :]
    if held:
        fresh_ref, part_ref = refs
    else:
        out_ref, part_ref, fresh_ref, out_sem = refs
    width = int_ref.shape[-1]
    middle = (present_ref.shape[1] - 1) // 2
    here = lax.axis_index("row")
    gap_column = gap_ref[...].T[:, :1]
    part = jnp.zeros(part_ref.shape, F32) if first else before_ref[...]
    stores = []
    items = [(lookup(slot, here), ref) for slot, ref in zip(slots, arrived)]
    if first:
        items.append((middle, None))
    for number, (index, ref) in enumerate(items):
        integ, mine = int_ref[0, index], kept_ref[index]
        if ref is None:
            theirs, gap_other = mine.T, gap_ref[:1, :]
        else:
            theirs = jnp.concatenate([ref[pl.ds(side * width, width), :].T for side in range(2)], axis=0)
            gap_other = jnp.concatenate([ref[pl.ds(2 * width + side, 1), :] for side in range(2)], axis=1)
        at_slot = lax.broadcasted_iota(jnp.int32, present_ref.shape, 1) == index
        flag = jnp.sum(jnp.where(at_slot, present_ref[...], 0), axis=1, keepdims=True)
        total = integ + mine + theirs
        fresh = jnp.where(flag > 0, total / (gap_column + gap_other), F32(0.0))
        fresh_ref[number] = fresh
        if not held:
            stores.append(pltpu.make_async_copy(fresh_ref.at[number], out_ref.at[0, index], out_sem.at[number]))
            stores[-1].start()
        part = part + jnp.sum((fresh * integ).reshape(width // 8, 8, width), axis=0)
    part_ref[...] = part
    for copy in stores:
        copy.wait()


def store_kernel(slots, _, *refs):
    *fresh, out_ref, out_sem = refs
    here = lax.axis_index("row")
    blocks = [ref.at[number] for ref in fresh for number in range(ref.shape[0])]
    stores = []
    for number, (slot, block) in enumerate(zip(slots, blocks)):
        stores.append(pltpu.make_async_copy(block, out_ref.at[0, lookup(slot, here)], out_sem.at[number]))
        stores[-1].start()
    for copy in stores:
        copy.wait()


PARAMS = pltpu.CompilerParams(vmem_limit_bytes=16 * 1024 * 1024)
IN_HBM = pl.BlockSpec(memory_space=pltpu.HBM)
IN_VMEM = pl.BlockSpec(memory_space=pltpu.VMEM)
DMA = pltpu.SemaphoreType.DMA
SMALL = pl.CostEstimate(flops=1, bytes_accessed=1, transcendentals=0)
CYCLES = (0, 2, 5, 8, 14)
UPDATES = (0, 5, 9, 10, 11, 12, 13, 14)
HELD = 1


def per_device(amplitude, integral, pair_gap, present):
    slots, width = amplitude.shape[1], amplitude.shape[2]
    reach = (slots - 1) // 2
    count = lax.axis_size("row")
    rounds, relays = rounds_of(count, reach)
    order = [turn[1] for turn in rounds] + [[reach]]

    def hbm(*values):
        return [pltpu.with_memory_space_constraint(value, pltpu.HBM) for value in values]

    def vmem(*values):
        return [pltpu.with_memory_space_constraint(value, pltpu.VMEM) for value in values]

    cube = pltpu.VMEM((slots, width, width), F32)
    block = pltpu.VMEM((2 * width + EXTRA, HALF), F32)
    first = CYCLES[1]
    gap, flags, kept, *sent = pl.pallas_call(
        functools.partial(first_kernel, order[:first]),
        in_specs=[IN_HBM] * 4,
        out_specs=[IN_VMEM] * (3 + first),
        out_shape=[pltpu.VMEM((EXTRA, width), F32), pltpu.VMEM(present.shape, present.dtype), cube]
        + [block] * first,
        scratch_shapes=[
            pltpu.VMEM((first, width, width), F32),
            pltpu.VMEM((first, width, width), F32),
            pltpu.VMEM((1, width), F32),
            DMA((first, 2)),
            DMA((2,)),
        ],
        compiler_params=PARAMS,
        cost_estimate=SMALL,
        name="first_blocks",
    )(*hbm(amplitude, integral, pair_gap, present))

    def cycles(start, stop, kept, arrived):
        passed = [(by, second - start, first) for _, by, _, first, second in relays if start <= second < stop]
        arrived = arrived if passed else []
        some = order[start:stop] + ([order[-1]] if stop == len(rounds) else [])
        kept, *sent = pl.pallas_call(
            functools.partial(cycle_kernel, some, passed, len(arrived)),
            in_specs=[IN_VMEM] * (4 + len(arrived)),
            out_specs=[IN_VMEM] * (1 + stop - start),
            out_shape=[cube] + [block] * (stop - start),
            input_output_aliases={3: 0},
            compiler_params=PARAMS,
            cost_estimate=SMALL,
            name="cycle_blocks",
        )(*vmem(amplitude, integral, gap, kept, *arrived))
        return kept, sent

    def send(start, stop):
        return [lax.ppermute(sent[number], "row", rounds[number][0]) for number in range(start, stop)]

    arrived = send(0, first)
    passing = 1 + max([hop for _, _, _, hop, _ in relays], default=-1)
    for start, stop in zip(CYCLES[1:-1], CYCLES[2:]):
        kept, more = cycles(start, stop, kept, arrived[:passing])
        sent += more
        arrived += send(start, stop)

    def updates(start, stop, held, before):
        some = [turn[2] for turn in rounds[start:stop]]
        first = start == 0
        n = len(some) + int(first)
        fresh = pltpu.VMEM((n, width, width), F32)
        part = pltpu.VMEM((8, width), F32)
        return pl.pallas_call(
            functools.partial(update_kernel, some, first, held),
            in_specs=[IN_VMEM] * (4 + len(some)) + ([] if first else [IN_VMEM] if held else [IN_HBM, IN_VMEM]),
            out_specs=[IN_VMEM if held else IN_HBM, IN_VMEM],
            out_shape=[fresh if held else pltpu.HBM((1, slots, width, width), F32), part],
            scratch_shapes=[] if held else [fresh, DMA((n,))],
            input_output_aliases={} if first or held else {4 + len(some): 0},
            compiler_params=PARAMS,
            cost_estimate=SMALL,
            name="held_update" if held else "update",
        )(
            *vmem(integral, gap, flags, kept, *arrived[start:stop]),
            *([] if first or held else hbm(before[0])),
            *([] if first else vmem(before[1])),
        )

    state, fresh = None, []
    for number, (start, stop) in enumerate(zip(UPDATES[:-1], UPDATES[1:])):
        state = updates(start, stop, number >= HELD, state)
        if number < HELD:
            updated = state[0]
        else:
            fresh.append(state[0])
    part = state[1]
    some = [turn[2] for turn in rounds[UPDATES[HELD] :]]
    updated = pl.pallas_call(
        functools.partial(store_kernel, some),
        in_specs=[IN_HBM] + [IN_VMEM] * len(fresh),
        out_specs=IN_HBM,
        out_shape=pltpu.HBM((1, slots, width, width), F32),
        scratch_shapes=[DMA((len(some),))],
        input_output_aliases={0: 0},
        compiler_params=PARAMS,
        cost_estimate=SMALL,
        name="store",
    )(*hbm(updated), *vmem(*fresh))

    summed = jnp.sum(part, axis=0).reshape(-1, 128).sum(axis=0)
    every = lax.all_to_all(jnp.broadcast_to(summed, (count, 128)), "row", 0, 0)
    blocks_all = count * amplitude.shape[0]
    energy = jnp.sum(every) / (width * width * blocks_all)
    return updated, jnp.reshape(energy, (1,))


def solution(mesh):
    in_specs = (
        P(("mol", "row"), None, None, None),
        P(("mol", "row"), None, None, None),
        P(("mol", "row"), None),
        P(("mol", "row"), None),
    )
    out_specs = (P(("mol", "row"), None, None, None), P("mol"))
    return jax.shard_map(per_device, mesh=mesh, in_specs=in_specs, out_specs=out_specs, check_vma=False)
```

```python
import functools

import jax
import jax.numpy as jnp
from jax import lax
from jax.experimental import pallas as pl
from jax.experimental.pallas import tpu as pltpu
from jax.sharding import PartitionSpec as P

F32 = jnp.float32
EXTRA = 8
HALF = 128

SENDS = (
    (7, 16, 6, 18, 21, 10, 9, 1, 3, 8, 4, 30, 31, 28, 13, 11),
    (6, 0, 19, -1, 21, 8, 11, 4, 12, 2, 13, 26, 9, -1, 7, 14),
    (4, 16, 7, -1, 8, 3, 13, 2, 6, 10, 11, 5, -1, 28, 31, 9),
    (2, 8, -1, 4, 6, 1, 3, 11, 10, 29, 14, 7, 5, -1, 9, 12),
    (17, 5, -1, 6, 7, 12, 4, 9, 2, 11, 3, 13, -1, 8, 31, 10),
    (19, 7, 22, 1, 16, 9, 18, 10, 5, 14, 15, 4, 8, 12, 27, 29),
    (5, 19, 1, 18, 10, 0, 7, 8, 9, 4, 6, 14, 15, 28, 11, 13),
    (17, 4, 19, 7, 9, 2, 8, 0, 11, 5, 12, 6, 29, 15, 10, 30),
    (-1, 3, 17, 2, 0, 4, 12, 5, 13, 7, 9, 10, 14, 11, 31, -1),
    (1, 6, 16, 5, 2, 11, 10, 3, 4, 15, 7, 12, 29, 9, 8, 30),
    (-1, 16, 4, 18, 5, 6, 1, 12, 14, 3, 27, 8, 13, 10, 15, -1),
    (3, -1, 5, 0, 1, 20, 2, 13, 7, 12, 8, 26, 11, 31, -1, 30),
    (17, -1, 0, 18, 3, 20, 5, 14, 15, 6, 27, 9, 10, 28, -1, 29),
    (20, 2, 3, 10, 11, 7, 0, 6, 1, 13, 5, 15, 25, 14, 12, 8),
)
RELAYS = (
    (3, 1, 8, 1, 12),
    (13, 15, 6, 1, 8),
    (3, 1, 9, 2, 11),
    (12, 14, 7, 2, 12),
    (2, 0, 9, 3, 10),
    (13, 15, 7, 3, 10),
    (2, 0, 8, 4, 8),
    (12, 14, 6, 4, 11),
)


def rounds_of(count, reach):
    rounds = []
    if count != len(SENDS[0]):
        for step in range(reach, 0, -1):
            for offset in (step, -step):
                pairs = [(row, (row + offset) % count) for row in range(count)]
                rounds.append((pairs, [reach + offset] * count, [reach - offset] * count))
        return rounds, ()
    for number, targets in enumerate(SENDS):
        pairs, sent, received = [], [None] * count, [None] * count
        for row, target in enumerate(targets):
            if target >= 0:
                pairs.append((row, target % count))
            if 0 <= target < count:
                sent[row], received[target] = reach + target - row, reach + row - target
        for origin, by, to, first, second in RELAYS:
            if number == first:
                pairs.append((origin, by))
                sent[origin] = reach + to - origin
            if number == second:
                pairs.append((by, to))
                received[to] = reach + origin - to
        rounds.append((pairs, sent, received))
    for row in range(count):
        for kind in (1, 2):
            used = {turn[kind][row] for turn in rounds}
            spare = [slot for slot in range(2 * reach + 1) if slot != reach and slot not in used]
            for turn in rounds:
                if turn[kind][row] is None:
                    turn[kind][row] = spare.pop()
    return rounds, RELAYS


def lookup(values, here):
    if len(set(values)) == 1:
        return values[0]
    words = [sum(value << 4 * place for place, value in enumerate(values[at : at + 8])) for at in (0, 8)]
    low, high = [word - 2**32 if word >= 2**31 else word for word in words]
    word = jnp.where(here < 8, jnp.int32(low), jnp.int32(high))
    return lax.shift_right_logical(word, 4 * lax.rem(here, 8)) & 15


def split(value):
    high = value.astype(jnp.bfloat16)
    low = (value - high.astype(F32)).astype(jnp.bfloat16)
    return high, low


def product(left, right):
    def one(a, b):
        return jnp.dot(a, b, preferred_element_type=F32)

    (left_high, left_low), (right_high, right_low) = left, right
    return one(left_high, right_high) + (one(left_high, right_low) + one(left_low, right_high))


def cycle_of(amp, integ):
    inner = product(split(integ), split(amp.T))
    inner = integ + integ.T - 0.5 * inner
    return product(split(amp), split(inner))


def halves(value):
    return [value[:, :HALF], value[:, HALF:]]


def put_cycle(amp, integ, gap_row, kept_ref, out_ref):
    cycle = cycle_of(amp, integ)
    kept_ref[...] = cycle
    if out_ref is not None:
        height = cycle.shape[0]
        for side, part in enumerate(halves(cycle)):
            out_ref[pl.ds(side * height, height), :] = part
        out_ref[pl.ds(2 * height, EXTRA), :] = jnp.concatenate(halves(gap_row) * (EXTRA // 2), axis=0)


def first_kernel(order, amp_hbm, int_hbm, gap_hbm, present_hbm, *refs):
    gap_ref, present_ref, kept_ref, *outs = refs[:-5]
    amp_buf, int_buf, gap_buf, block_sem, small_sem = refs[-5:]
    here = lax.axis_index("row")
    places = [lookup(slot, here) for slot in order]
    loads = []
    for number, index in enumerate(places):
        loads.append(pltpu.make_async_copy(amp_hbm.at[0, index], amp_buf.at[number], block_sem.at[number, 0]))
        loads.append(pltpu.make_async_copy(int_hbm.at[0, index], int_buf.at[number], block_sem.at[number, 1]))
        loads[-2].start()
        loads[-1].start()
    loads.append(pltpu.make_async_copy(gap_hbm, gap_buf, small_sem.at[0]))
    loads.append(pltpu.make_async_copy(present_hbm, present_ref, small_sem.at[1]))
    loads[-2].start()
    loads[-1].start()
    for copy in loads:
        copy.wait()
    gap_ref[...] = jnp.broadcast_to(gap_buf[...], gap_ref.shape)
    for number, index in enumerate(places):
        put_cycle(amp_buf[number], int_buf[number], gap_buf[...], kept_ref.at[index], outs[number])


def cycle_kernel(order, amp_ref, int_ref, gap_ref, _, kept_ref, *outs):
    here = lax.axis_index("row")
    for slot, out_ref in zip(order, [*outs, None]):
        index = lookup(slot, here)
        put_cycle(amp_ref[0, index], int_ref[0, index], gap_ref[:1, :], kept_ref.at[index], out_ref)


def relay_kernel(relays, arrays, *refs):
    arrived, outs = refs[:arrays], refs[arrays + (len(refs) - arrays) // 2 :]
    here = lax.axis_index("row")
    for row, output, array in relays:

        @pl.when(here == row)
        def _():
            outs[output][...] = arrived[array][...]


def update_kernel(slots, first, held, int_ref, gap_ref, present_ref, kept_ref, *refs):
    arrived, refs = refs[: len(slots)], refs[len(slots) :]
    if not first:
        before_ref, refs = refs[-3 - 2 * (not held)], refs[-2 - 2 * (not held) :]
    if held:
        fresh_ref, part_ref = refs
    else:
        out_ref, part_ref, fresh_ref, out_sem = refs
    width = int_ref.shape[-1]
    middle = (present_ref.shape[1] - 1) // 2
    here = lax.axis_index("row")
    gap_column = gap_ref[...].T[:, :1]
    part = jnp.zeros(part_ref.shape, F32) if first else before_ref[...]
    stores = []
    items = [(lookup(slot, here), ref) for slot, ref in zip(slots, arrived)]
    if first:
        items.append((middle, None))
    for number, (index, ref) in enumerate(items):
        integ, mine = int_ref[0, index], kept_ref[index]
        if ref is None:
            theirs, gap_other = mine.T, gap_ref[:1, :]
        else:
            theirs = jnp.concatenate([ref[pl.ds(side * width, width), :].T for side in range(2)], axis=0)
            gap_other = jnp.concatenate([ref[pl.ds(2 * width + side, 1), :] for side in range(2)], axis=1)
        at_slot = lax.broadcasted_iota(jnp.int32, present_ref.shape, 1) == index
        flag = jnp.sum(jnp.where(at_slot, present_ref[...], 0), axis=1, keepdims=True)
        total = integ + mine + theirs
        fresh = jnp.where(flag > 0, total / (gap_column + gap_other), F32(0.0))
        fresh_ref[number] = fresh
        if not held:
            stores.append(pltpu.make_async_copy(fresh_ref.at[number], out_ref.at[0, index], out_sem.at[number]))
            stores[-1].start()
        part = part + jnp.sum((fresh * integ).reshape(width // 8, 8, width), axis=0)
    part_ref[...] = part
    for copy in stores:
        copy.wait()


def store_kernel(slots, _, *refs):
    *fresh, out_ref, out_sem = refs
    here = lax.axis_index("row")
    blocks = [ref.at[number] for ref in fresh for number in range(ref.shape[0])]
    stores = []
    for number, (slot, block) in enumerate(zip(slots, blocks)):
        stores.append(pltpu.make_async_copy(block, out_ref.at[0, lookup(slot, here)], out_sem.at[number]))
        stores[-1].start()
    for copy in stores:
        copy.wait()


PARAMS = pltpu.CompilerParams(vmem_limit_bytes=16 * 1024 * 1024)
IN_HBM = pl.BlockSpec(memory_space=pltpu.HBM)
IN_VMEM = pl.BlockSpec(memory_space=pltpu.VMEM)
DMA = pltpu.SemaphoreType.DMA
SMALL = pl.CostEstimate(flops=1, bytes_accessed=1, transcendentals=0)
CYCLES = (0, 2, 5, 8, 14)
UPDATES = (0, 5, 9, 10, 11, 12, 13, 14)
HELD = 1


def per_device(amplitude, integral, pair_gap, present):
    slots, width = amplitude.shape[1], amplitude.shape[2]
    reach = (slots - 1) // 2
    count = lax.axis_size("row")
    rounds, relays = rounds_of(count, reach)
    order = [turn[1] for turn in rounds] + [[reach]]

    def hbm(*values):
        return [pltpu.with_memory_space_constraint(value, pltpu.HBM) for value in values]

    def vmem(*values):
        return [pltpu.with_memory_space_constraint(value, pltpu.VMEM) for value in values]

    cube = pltpu.VMEM((slots, width, width), F32)
    block = pltpu.VMEM((2 * width + EXTRA, HALF), F32)
    first = CYCLES[1]
    gap, flags, kept, *sent = pl.pallas_call(
        functools.partial(first_kernel, order[:first]),
        in_specs=[IN_HBM] * 4,
        out_specs=[IN_VMEM] * (3 + first),
        out_shape=[pltpu.VMEM((EXTRA, width), F32), pltpu.VMEM(present.shape, present.dtype), cube]
        + [block] * first,
        scratch_shapes=[
            pltpu.VMEM((first, width, width), F32),
            pltpu.VMEM((first, width, width), F32),
            pltpu.VMEM((1, width), F32),
            DMA((first, 2)),
            DMA((2,)),
        ],
        compiler_params=PARAMS,
        cost_estimate=SMALL,
        name="first_blocks",
    )(*hbm(amplitude, integral, pair_gap, present))

    def cycles(start, stop, kept):
        some = order[start:stop] + ([order[-1]] if stop == len(rounds) else [])
        kept, *sent = pl.pallas_call(
            functools.partial(cycle_kernel, some),
            in_specs=[IN_VMEM] * 4,
            out_specs=[IN_VMEM] * (1 + stop - start),
            out_shape=[cube] + [block] * (stop - start),
            input_output_aliases={3: 0},
            compiler_params=PARAMS,
            cost_estimate=SMALL,
            name="cycle_blocks",
        )(*vmem(amplitude, integral, gap, kept))
        return kept, sent

    def relayed(arrived, start, sent):
        passed = [(by, second - start, first) for _, by, _, first, second in relays]
        if not passed:
            return sent
        arrived = arrived[: 1 + max(first for _, _, first in passed)]
        return pl.pallas_call(
            functools.partial(relay_kernel, passed, len(arrived)),
            in_specs=[IN_VMEM] * (len(arrived) + len(sent)),
            out_specs=[IN_VMEM] * len(sent),
            out_shape=[block] * len(sent),
            input_output_aliases={len(arrived) + number: number for number in range(len(sent))},
            compiler_params=PARAMS,
            cost_estimate=SMALL,
            name="relayed_blocks",
        )(*vmem(*arrived, *sent))

    def send(start, stop):
        return [lax.ppermute(sent[number], "row", rounds[number][0]) for number in range(start, stop)]

    arrived = send(0, first)
    for start, stop in zip(CYCLES[1:-1], CYCLES[2:]):
        kept, more = cycles(start, stop, kept)
        sent += relayed(arrived, start, more) if stop == len(rounds) else more
        arrived += send(start, stop)

    def updates(start, stop, held, before):
        some = [turn[2] for turn in rounds[start:stop]]
        first = start == 0
        n = len(some) + int(first)
        fresh = pltpu.VMEM((n, width, width), F32)
        part = pltpu.VMEM((8, width), F32)
        return pl.pallas_call(
            functools.partial(update_kernel, some, first, held),
            in_specs=[IN_VMEM] * (4 + len(some)) + ([] if first else [IN_VMEM] if held else [IN_HBM, IN_VMEM]),
            out_specs=[IN_VMEM if held else IN_HBM, IN_VMEM],
            out_shape=[fresh if held else pltpu.HBM((1, slots, width, width), F32), part],
            scratch_shapes=[] if held else [fresh, DMA((n,))],
            input_output_aliases={} if first or held else {4 + len(some): 0},
            compiler_params=PARAMS,
            cost_estimate=SMALL,
            name="held_update" if held else "update",
        )(
            *vmem(integral, gap, flags, kept, *arrived[start:stop]),
            *([] if first or held else hbm(before[0])),
            *([] if first else vmem(before[1])),
        )

    state, fresh = None, []
    for number, (start, stop) in enumerate(zip(UPDATES[:-1], UPDATES[1:])):
        state = updates(start, stop, number >= HELD, state)
        if number < HELD:
            updated = state[0]
        else:
            fresh.append(state[0])
    part = state[1]
    some = [turn[2] for turn in rounds[UPDATES[HELD] :]]
    updated = pl.pallas_call(
        functools.partial(store_kernel, some),
        in_specs=[IN_HBM] + [IN_VMEM] * len(fresh),
        out_specs=IN_HBM,
        out_shape=pltpu.HBM((1, slots, width, width), F32),
        scratch_shapes=[DMA((len(some),))],
        input_output_aliases={0: 0},
        compiler_params=PARAMS,
        cost_estimate=SMALL,
        name="store",
    )(*hbm(updated), *vmem(*fresh))

    summed = jnp.sum(part, axis=0).reshape(-1, 128).sum(axis=0)
    every = lax.all_to_all(jnp.broadcast_to(summed, (count, 128)), "row", 0, 0)
    blocks_all = count * amplitude.shape[0]
    energy = jnp.sum(every) / (width * width * blocks_all)
    return updated, jnp.reshape(energy, (1,))


def solution(mesh):
    in_specs = (
        P(("mol", "row"), None, None, None),
        P(("mol", "row"), None, None, None),
        P(("mol", "row"), None),
        P(("mol", "row"), None),
    )
    out_specs = (P(("mol", "row"), None, None, None), P("mol"))
    return jax.shard_map(per_device, mesh=mesh, in_specs=in_specs, out_specs=out_specs, check_vma=False)
```
